32 devices in a mesh: shot: 2 (over y), gx: 4 (over z), section: 2 (over x), gy: 2 (over core).
Axes of the slice: x: 2, y: 2, z: 4, core: 2. Of those that a mesh axis runs over, the one named last changes fastest.
Arguments:
- wave_now: float32 [256, 32, 512], P(('shot', 'gx'), 'section', 'gy'), parts along dimension 0, may hold values from -6 to 6
- wave_before: float32 [256, 32, 512], P(('shot', 'gx'), 'section', 'gy'), parts along dimension 0, may hold values from -6 to 6
- courant: float32 [256, 32, 512], P(('shot', 'gx'), 'section', 'gy'), parts along dimension 0, may hold values from 0.03 to 0.12
- anisotropy: float32 [256, 32, 512], P(('shot', 'gx'), 'section', 'gy'), parts along dimension 0, may hold values from 0 to 0.3
- tilt: float32 [256, 32, 512], P(('shot', 'gx'), 'section', 'gy'), parts along dimension 0, may hold values from -3.140625 to 3.140625
- reflectivity: bfloat16 [17, 256, 32, 512], P(None, ('shot', 'gx'), 'section', 'gy'), parts along dimension 1, may hold values from -2.5 to 2.5
- offsets: int32 [17], replicated, may hold values from -16 to 16, as said below
Outputs:
- background: float32 [256, 32, 512], P(('shot', 'gx'), 'section', 'gy'), parts along dimension 0
- scattered: float32 [256, 32, 512], P(('shot', 'gx'), 'section', 'gy'), parts along dimension 0
The draws below stay inside these ranges and needn't reach their ends.
There are 2 independent parts, one for each index of `shot`. The reference program is written for one: setup_inputs(seed, part) draws one part's arguments, and reference() takes and returns one part's arrays. A program takes and returns all parts, laid end to end along the dimension named above; an argument that names none is the same for every part. Nothing has to cross between parts.
Inputs may be any that keep to these rules, and one draw needn't show every extreme that they name: 17 distinct offsets, among them 0, -16 and 16.
All inputs are finite; a program needn't handle non-finite values.
Results may differ from the reference program's by a relative error of at most 0.0003.
Values sent between devices are 32-bit elements; how exact they have to be, the bound alone decides.
A program may use at most 64 MiB of HBM per device.

```python
import math
import jax
import jax.numpy as jnp
from jax import lax

NOFF = 17
MARGIN = 16
ROUNDS = 3
STEPS = 2
NX = 128
NZ = 32
NY = 512


def draw_offsets(key, part):
    inside_values = jnp.concatenate([jnp.arange(1 - MARGIN, 0), jnp.arange(1, MARGIN)]).astype(jnp.int32)
    key_pick, key_order = jax.random.split(jax.random.fold_in(key, 11))
    chosen = jax.random.permutation(key_pick, inside_values)[:NOFF - 3]
    end_values = jnp.array([-MARGIN, 0, MARGIN], jnp.int32)
    return jax.random.permutation(key_order, jnp.concatenate([end_values, chosen])).astype(jnp.int32)


def block_levels(own_key, extent, cuts, least, top_value):
    factor_of, own = 1.0, jax.random.fold_in(own_key, 6)
    for position, parts in cuts:
        draws = jnp.exp(jax.random.uniform(jax.random.fold_in(own, position), (parts,), jnp.float32, least / len(cuts), top_value / len(cuts)))
        factor_of = factor_of * jnp.repeat(draws, extent[position] // parts).reshape([-1 if axis == position else 1 for axis in range(len(extent))])
    return factor_of


def noise(own_key, shape, deviation, limit, shards=(), dtype=jnp.bfloat16):
    level = block_levels(own_key, shape, shards, -0.22, 0.18) if shards else 1.0
    values = jax.random.normal(own_key, shape, jnp.float32) * deviation * level
    return jnp.minimum(jnp.maximum(values, -limit), limit).astype(dtype)


def setup_inputs(seed: int = 0, part: int = 0) -> dict:
    streams_of = jax.random.split(jax.random.key(seed), 8)
    part_keys = jax.random.split(jax.random.fold_in(streams_of[7], part), 8)
    wave_now = noise(part_keys[0], (NX, NZ, NY), 1.0, 6.0, ((0, 4), (1, 2), (2, 2)), jnp.float32)
    wave_before = noise(part_keys[1], (NX, NZ, NY), 1.0, 6.0, ((0, 4), (1, 2), (2, 2)), jnp.float32)
    courant = jnp.clip(jnp.exp(math.log(0.12) - 1.3862944 * jax.random.uniform(part_keys[2], (NX, NZ, NY), jnp.float32) ** block_levels(part_keys[2], (NX, NZ, NY), ((0, 4), (1, 2), (2, 2)), -0.2, 0.2)), 0.03, 0.12)
    anisotropy = jnp.clip(0.3 * jax.random.uniform(part_keys[3], (NX, NZ, NY), jnp.float32) ** block_levels(part_keys[3], (NX, NZ, NY), ((0, 4), (1, 2), (2, 2)), -0.2, 0.2), 0.0, 0.3)
    tilt = jnp.clip(jax.random.uniform(part_keys[4], (NX, NZ, NY), jnp.float32, -3.140625, 3.140625), -3.140625, 3.140625)
    reflectivity = noise(part_keys[5], (NOFF, NX, NZ, NY), 0.25, 2.5, ((1, 4), (2, 2), (3, 2)))
    offsets = draw_offsets(jax.random.fold_in(streams_of[7], 71), part)
    return {"wave_now": wave_now, "wave_before": wave_before, "courant": courant, "anisotropy": anisotropy, "tilt": tilt, "reflectivity": reflectivity, "offsets": offsets}


def coefficients(courant, anisotropy, tilt):
    sine_tilt = jnp.sin(tilt)
    cosine_tilt = jnp.cos(tilt)
    stretch = 1.0 + 2.0 * anisotropy
    coef_xx = courant * (stretch * cosine_tilt * cosine_tilt + sine_tilt * sine_tilt)
    coef_zz = courant * (stretch * sine_tilt * sine_tilt + cosine_tilt * cosine_tilt)
    coef_yy = courant * stretch
    coef_xz = courant * 4.0 * anisotropy * sine_tilt * cosine_tilt
    return coef_xx, coef_zz, coef_yy, coef_xz


def apply_operator(padded, coef_set):
    centre = padded[1:-1, 1:-1, 1:-1]
    diff_xx = padded[2:, 1:-1, 1:-1] + padded[:-2, 1:-1, 1:-1] - 2.0 * centre
    diff_zz = padded[1:-1, 2:, 1:-1] + padded[1:-1, :-2, 1:-1] - 2.0 * centre
    diff_yy = padded[1:-1, 1:-1, 2:] + padded[1:-1, 1:-1, :-2] - 2.0 * centre
    diff_xz = 0.25 * (padded[2:, 2:, 1:-1] - padded[2:, :-2, 1:-1] - padded[:-2, 2:, 1:-1] + padded[:-2, :-2, 1:-1])
    return coef_set[0] * diff_xx + coef_set[1] * diff_zz + coef_set[2] * diff_yy + coef_set[3] * diff_xz


def reference(wave_now, wave_before, courant, anisotropy, tilt, reflectivity, offsets):
    coef_set = coefficients(courant, anisotropy, tilt)
    current = wave_now
    prior = wave_before
    wave_scat = jnp.zeros_like(wave_now)
    scat_prior = jnp.zeros_like(wave_now)
    for round_index in range(ROUNDS):
        for step_index in range(STEPS):
            advanced = 2.0 * current - prior + apply_operator(jnp.pad(current, 1), coef_set)
            prior = current
            current = advanced
        extended = jnp.pad(current, ((MARGIN, MARGIN), (0, 0), (0, 0)))

        def accumulate(offset_index, running):
            start = (MARGIN + offsets[offset_index]).astype(jnp.int32)
            moved = lax.dynamic_slice_in_dim(extended, start, current.shape[0], 0)
            return running + reflectivity[offset_index].astype(jnp.float32) * moved

        source = lax.fori_loop(0, NOFF, accumulate, jnp.zeros_like(current))
        forcing = courant * source
        for step_index in range(STEPS):
            advanced = 2.0 * wave_scat - scat_prior + apply_operator(jnp.pad(wave_scat, 1), coef_set) + forcing
            scat_prior = wave_scat
            wave_scat = advanced
    return current, wave_scat
```

```python
import functools

import jax
import jax.numpy as jnp
from jax import lax
from jax.experimental import pallas as pl
from jax.experimental.pallas import tpu as pltpu
from jax.sharding import PartitionSpec as P

MARGIN = 16
LANES = 128
Z0 = 8
MESH = pl.DeviceIdType.MESH
DIAGONALS = ((1, 1), (1, -1), (-1, 1), (-1, -1))
X_UP, X_DOWN, FAR_UP, FAR_DOWN, Z_UP, Z_DOWN, SIDE, DIAG = 0, 1, 2, 3, 4, 5, 6, 7
SLOTS = 11

PI_HIGH = 3.140625
PI_LOW = 9.67653589793e-4


def trig_products(tilt):
    turns = jnp.round(tilt * (1.0 / 3.14159265358979))
    t = tilt - turns * PI_HIGH
    t = t - turns * PI_LOW
    q = t * t
    s = -2.5052108e-08
    for c in (2.7557319e-06, -1.9841270e-04, 8.3333333e-03, -1.6666667e-01, 1.0):
        s = s * q + c
    s = s * t
    c_ = 2.0876757e-09
    for c in (-2.7557319e-07, 2.4801587e-05, -1.3888889e-03, 4.1666667e-02, -0.5, 1.0):
        c_ = c_ * q + c
    return s * s, c_ * c_, s * c_


def kernel(
    n_gx, n_sec, n_gy, noff,
    now_h, before_h, courant_h, aniso_h, tilt_h, refl_h, off_s,
    back_h, scat_h,
    u0, u1, u2, u3, u4, u5, u6, w1, w2, w3, w4, w5, before, coef, courant, refl, force, last,
    in_sem, out_sem, send_sem, recv_sem,
):
    X, Z = before.shape[1], before.shape[2]
    NT = before.shape[0]
    shot, gx, sec, gy = (lax.axis_index(a) for a in ("shot", "gx", "section", "gy"))
    partner = n_gy - 1 - gy
    rows = pl.ds(Z0, Z)

    def there(dx, dz):
        ok = None
        for d, i, n in ((dx, gx, n_gx), (dz, sec, n_sec)):
            if d:
                here = (i + d >= 0) & (i + d < n)
                ok = here if ok is None else ok & here
        return ok

    def device(dx, dz):
        return (shot, lax.rem(gx + dx + n_gx, n_gx), lax.rem(sec + dz + n_sec, n_sec), gy)

    side_device = (shot, gx, sec, partner)
    moves = ((1, 0), (-1, 0), (0, 1), (0, -1)) + DIAGONALS

    barrier = pltpu.get_barrier_semaphore()
    count = jnp.int32(1)
    for dx, dz in moves:
        ok = there(dx, dz)
        count += ok.astype(jnp.int32)

        @pl.when(ok)
        def _():
            pl.semaphore_signal(barrier, inc=1, device_id=device(dx, dz), device_id_type=MESH)

    pl.semaphore_signal(barrier, inc=1, device_id=side_device, device_id_type=MESH)

    def load(source, target, i):
        out = []
        for t in range(NT):
            c = pltpu.make_async_copy(
                source.at[:, :, pl.ds(t * LANES, LANES)], target(t), in_sem.at[i * NT + t]
            )
            c.start()
            out.append(c)
        return out

    ins = [
        load(now_h, lambda t: u0.at[t, pl.ds(1, X), rows, :], 0),
        load(tilt_h, lambda t: coef.at[0, t], 1),
        load(aniso_h, lambda t: coef.at[1, t], 2),
        load(courant_h, lambda t: courant.at[t], 3),
        load(before_h, lambda t: before.at[t], 4),
    ]
    refl_in = []
    for t in range(NT):
        c = pltpu.make_async_copy(
            refl_h.at[:, :, :, pl.ds(t * LANES, LANES)], refl.at[t], in_sem.at[5 * NT + t]
        )
        c.start()
        refl_in.append(c)

    def remote(src, dst, e, slot, dev):
        return pltpu.make_async_remote_copy(
            src_ref=src, dst_ref=dst,
            send_sem=send_sem.at[e * SLOTS + slot], recv_sem=recv_sem.at[e * SLOTS + slot],
            device_id=dev, device_id_type=MESH,
        )

    def pad_of(f):
        return (f.shape[1] - X) // 2

    def exchange(f, e, near=True, far=False, skip=0):
        px = pad_of(f)
        every = pl.ds(0, NT)
        xs = pl.ds(px, X)
        out = []
        if near:
            for d, slot in ((1, X_UP), (-1, X_DOWN)):
                src = px + X - 1 if d == 1 else px
                dst = px - 1 if d == 1 else px + X
                out.append((there(d, 0), there(-d, 0), remote(
                    f.at[every, pl.ds(src, 1), rows, :], f.at[every, pl.ds(dst, 1), rows, :],
                    e, slot, device(d, 0))))
            for d, slot in ((1, Z_UP), (-1, Z_DOWN)):
                src = Z0 + Z - 1 if d == 1 else Z0
                dst = Z0 - 1 if d == 1 else Z0 + Z
                out.append((there(0, d), there(0, -d), remote(
                    f.at[every, xs, pl.ds(src, 1), :], f.at[every, xs, pl.ds(dst, 1), :],
                    e, slot, device(0, d))))
            for k, (dx, dz) in enumerate(DIAGONALS):
                sx, tx = (px + X - 1, px - 1) if dx == 1 else (px, px + X)
                sz, tz = (Z0 + Z - 1, Z0 - 1) if dz == 1 else (Z0, Z0 + Z)
                out.append((there(dx, dz), there(-dx, -dz), remote(
                    f.at[every, pl.ds(sx, 1), pl.ds(sz, 1), :],
                    f.at[every, pl.ds(tx, 1), pl.ds(tz, 1), :],
                    e, DIAG + k, device(dx, dz))))
            out.append((None, None, remote(
                f.at[(NT - 1) * (1 - gy), xs, rows, :], f.at[NT, xs, rows, :],
                e, SIDE, side_device)))
        if far:
            size = MARGIN - skip
            for d, slot in ((1, FAR_UP), (-1, FAR_DOWN)):
                src = px + X - MARGIN if d == 1 else px + skip
                dst = px - MARGIN if d == 1 else px + X + skip
                out.append((there(d, 0), there(-d, 0), remote(
                    f.at[every, pl.ds(src, size), rows, :], f.at[every, pl.ds(dst, size), rows, :],
                    e, slot, device(d, 0))))
        return out

    def guarded(ok, act):
        if ok is None:
            act()
        else:
            pl.when(ok)(act)

    sent = []

    def send(copies):
        for ok, _, c in copies:
            guarded(ok, lambda c=c: c.start())
        sent.append(copies)
        return copies

    def receive(copies):
        for _, ok, c in copies:
            guarded(ok, lambda c=c: c.wait_recv())

    def clear(f, near=True):
        px = pad_of(f)
        deep = px
        for d in (1, -1):
            @pl.when(jnp.logical_not(there(d, 0)))
            def _():
                start = px + X if d == 1 else 0

                @pl.loop(0, deep)
                def _(i):
                    for t in range(NT):
                        f[t, start + i] = jnp.zeros(f.shape[2:], f.dtype)

            if near:
                @pl.when(jnp.logical_not(there(0, d)))
                def _():
                    row = Z0 + Z if d == 1 else Z0 - 1

                    @pl.loop(0, X + 2)
                    def _(i):
                        for t in range(NT):
                            f[t, px - 1 + i, pl.ds(row, 1), :] = jnp.zeros((1, LANES), f.dtype)

    lane = lax.broadcasted_iota(jnp.int32, (Z, LANES), 1)
    first, final = lane == 0, lane == LANES - 1
    has_left = jnp.full((Z, LANES), gy, jnp.int32) > 0
    turn = 1 + (LANES - 2) * (1 - gy)

    def step(f, prior, out, forcing=None):
        px = pad_of(f)

        def plane(i):
            c, s, d = [], [], []
            for t in range(NT):
                c.append(f[t, i, rows, :])
                hi = f[t, i, pl.ds(Z0 + 1, Z), :]
                lo = f[t, i, pl.ds(Z0 - 1, Z), :]
                s.append(hi + lo)
                d.append(hi - lo)
            return c, s, d

        def body(x, carry):
            cm, dm, c, s, d = carry
            cp, sp, dp = plane(px + x + 1)
            up = [pltpu.roll(v, 1, 1) for v in c]
            down = [pltpu.roll(v, LANES - 1, 1) for v in c]
            edge = pltpu.roll(f[NT, px + x, rows, :], turn, 1)
            edge_l = jnp.where(has_left, edge, 0.0)
            edge_r = jnp.where(has_left, 0.0, edge)
            for t in range(NT):
                left = jnp.where(first, up[t - 1] if t else edge_l, up[t])
                right = jnp.where(final, down[t + 1] if t < NT - 1 else edge_r, down[t])
                v = coef[0, t, x] * (cp[t] + cm[t])
                v += coef[1, t, x] * s[t]
                v += coef[2, t, x] * (left + right)
                v += coef[3, t, x] * (dp[t] - dm[t])
                v += coef[4, t, x] * c[t]
                if prior is not None:
                    v -= prior(t, x)
                if forcing is not None:
                    v += forcing(t, x)
                out(t, x, v)
            return c, d, cp, sp, dp

        cm, _, dm = plane(px - 1)
        c, s, d = plane(px)
        lax.fori_loop(0, X, body, (cm, dm, c, s, d), unroll=2)

    def reader(f):
        px = pad_of(f)
        return lambda t, x: f[t, px + x, rows, :]

    def writer(f):
        px = pad_of(f)

        def put(t, x, v):
            f[t, px + x, rows, :] = v

        return put

    def source(f, out):
        px = pad_of(f)
        starts = [off_s[h] + px for h in range(noff)]

        def body(x, carry):
            for t in range(NT):
                total = jnp.zeros((Z, LANES), jnp.float32)
                for h in range(noff):
                    total += refl[t, h, x].astype(jnp.float32) * f[t, x + starts[h], rows, :]
                out(t, x, courant[t, x] * total)
            return carry

        lax.fori_loop(0, X, body, 0)

    def plain(f):
        return lambda t, x: f[t, x]

    def put_plain(f):
        def put(t, x, v):
            f[t, x] = v

        return put

    for c in ins[0]:
        c.wait()
    pl.semaphore_wait(barrier, count)
    e0 = send(exchange(u0, 0))
    for k in (1, 2, 3, 4):
        for c in ins[k]:
            c.wait()

    def coefficients(x, carry):
        for t in range(NT):
            ss, cc, sc = trig_products(coef[0, t, x])
            e = coef[1, t, x]
            k = courant[t, x]
            stretch = 1.0 + 2.0 * e
            xx = k * (stretch * cc + ss)
            zz = k * (stretch * ss + cc)
            yy = k * stretch
            coef[0, t, x] = xx
            coef[1, t, x] = zz
            coef[2, t, x] = yy
            coef[3, t, x] = k * e * sc
            coef[4, t, x] = 2.0 - 2.0 * (xx + zz + yy)
        return carry

    lax.fori_loop(0, X, coefficients, 0, unroll=2)
    for f in (u0, u1, u2, u3, u4, u5, w1, w2, w3, w4, w5):
        clear(f)
    clear(u6, near=False)

    receive(e0)
    step(u0, plain(before), writer(u1))
    e1 = send(exchange(u1, 1))
    receive(e1)
    step(u1, reader(u0), writer(u2))
    e2 = send(exchange(u2, 2))
    far2 = send(exchange(u2, 2, near=False, far=True, skip=1))
    receive(e2)
    step(u2, reader(u1), writer(u3))
    e3 = send(exchange(u3, 3))
    for c in refl_in:
        c.wait()
    receive(e3)
    step(u3, reader(u2), writer(u4))
    e4 = send(exchange(u4, 4))
    far4 = send(exchange(u4, 4, near=False, far=True, skip=1))
    receive(far2)
    source(u2, writer(w1))
    g1 = send(exchange(w1, 7))
    receive(e4)
    step(u4, reader(u3), writer(u5))
    e5 = send(exchange(u5, 5))
    receive(g1)
    step(w1, None, writer(w2), reader(w1))
    g2 = send(exchange(w2, 8))
    receive(e5)
    step(u5, reader(u4), writer(u6))
    far6 = send(exchange(u6, 6, near=False, far=True))
    outs = []
    for t in range(NT):
        c = pltpu.make_async_copy(
            u6.at[t, pl.ds(MARGIN, X), rows, :], back_h.at[:, :, pl.ds(t * LANES, LANES)], out_sem.at[t]
        )
        c.start()
        outs.append(c)
    receive(far4)
    source(u4, put_plain(force))
    receive(g2)
    step(w2, reader(w1), writer(w3), plain(force))
    g3 = send(exchange(w3, 9))
    receive(g3)
    step(w3, reader(w2), writer(w4), plain(force))
    g4 = send(exchange(w4, 10))
    receive(far6)
    source(u6, put_plain(force))
    receive(g4)
    step(w4, reader(w3), writer(w5), plain(force))
    g5 = send(exchange(w5, 11))
    receive(g5)
    step(w5, reader(w4), put_plain(last), plain(force))
    for t in range(NT):
        c = pltpu.make_async_copy(
            last.at[t], scat_h.at[:, :, pl.ds(t * LANES, LANES)], out_sem.at[NT + t]
        )
        c.start()
        outs.append(c)
    for copies in sent:
        for ok, _, c in copies:
            guarded(ok, lambda c=c: c.wait_send())
    for c in outs:
        c.wait()


def shards(sizes, wave_now, wave_before, courant, anisotropy, tilt, reflectivity, offsets):
    X, Z, Y = wave_now.shape
    noff = reflectivity.shape[0]
    NT = Y // LANES
    f32 = jnp.float32
    thin = pltpu.VMEM((NT + 1, X + 2, Z + 2 * Z0, LANES), f32)
    wide = pltpu.VMEM((NT + 1, X + 2 * MARGIN, Z + 2 * Z0, LANES), f32)
    block = pltpu.VMEM((NT, X, Z, LANES), f32)
    exchanges = 12
    any_ = pl.BlockSpec(memory_space=pl.ANY)
    shape = jax.ShapeDtypeStruct(wave_now.shape, f32)
    return pl.pallas_call(
        functools.partial(kernel, *sizes, noff),
        out_shape=(shape, shape),
        in_specs=[any_] * 6 + [pl.BlockSpec(memory_space=pltpu.SMEM)],
        out_specs=(any_, any_),
        scratch_shapes=[
            thin, thin, wide, thin, wide, thin, wide,
            thin, thin, thin, thin, thin,
            block,
            pltpu.VMEM((5, NT, X, Z, LANES), f32),
            block,
            pltpu.VMEM((NT, noff, X, Z, LANES), jnp.bfloat16),
            block, block,
            pltpu.SemaphoreType.DMA((6 * NT,)),
            pltpu.SemaphoreType.DMA((2 * NT,)),
            pltpu.SemaphoreType.DMA((exchanges * SLOTS,)),
            pltpu.SemaphoreType.DMA((exchanges * SLOTS,)),
        ],
        compiler_params=pltpu.CompilerParams(
            collective_id=0, has_side_effects=True, vmem_limit_bytes=56 * 1024 * 1024
        ),
    )(wave_now, wave_before, courant, anisotropy, tilt, reflectivity, offsets)


def solution(mesh):
    field = P(("shot", "gx"), "section", "gy")
    sizes = tuple(mesh.shape[a] for a in ("gx", "section", "gy"))
    return jax.shard_map(
        functools.partial(shards, sizes),
        mesh=mesh,
        in_specs=(field, field, field, field, field, P(None, ("shot", "gx"), "section", "gy"), P()),
        out_specs=(field, field),
        check_vma=False,
    )
```

```python
import functools

import jax
import jax.numpy as jnp
from jax import lax
from jax.experimental import pallas as pl
from jax.experimental.pallas import tpu as pltpu
from jax.sharding import PartitionSpec as P

MARGIN = 16
LANES = 128
Z0 = 8
MESH = pl.DeviceIdType.MESH
DIAGONALS = ((1, 1), (1, -1), (-1, 1), (-1, -1))
X_UP, X_DOWN, FAR_UP, FAR_DOWN, Z_UP, Z_DOWN, SIDE, DIAG = 0, 1, 2, 3, 4, 5, 6, 7
SLOTS = 11

PI_HIGH = 3.140625
PI_LOW = 9.67653589793e-4


def trig_products(tilt):
    turns = jnp.round(tilt * (1.0 / 3.14159265358979))
    t = tilt - turns * PI_HIGH
    t = t - turns * PI_LOW
    q = t * t
    s = -2.5052108e-08
    for c in (2.7557319e-06, -1.9841270e-04, 8.3333333e-03, -1.6666667e-01, 1.0):
        s = s * q + c
    s = s * t
    c_ = 2.0876757e-09
    for c in (-2.7557319e-07, 2.4801587e-05, -1.3888889e-03, 4.1666667e-02, -0.5, 1.0):
        c_ = c_ * q + c
    return s * s, c_ * c_, s * c_


def kernel(
    n_gx, n_sec, n_gy, noff,
    now_h, before_h, courant_h, aniso_h, tilt_h, refl_h, off_s,
    back_h, scat_h,
    u0, u1, u2, u3, u4, u5, u6, w1, w2, w3, w4, w5, before, coef, courant, refl, force, last,
    in_sem, out_sem, send_sem, recv_sem,
):
    X, Z = before.shape[1], before.shape[2]
    NT = before.shape[0]
    shot, gx, sec, gy = (lax.axis_index(a) for a in ("shot", "gx", "section", "gy"))
    partner = n_gy - 1 - gy
    rows = pl.ds(Z0, Z)

    def there(dx, dz):
        ok = None
        for d, i, n in ((dx, gx, n_gx), (dz, sec, n_sec)):
            if d:
                here = (i + d >= 0) & (i + d < n)
                ok = here if ok is None else ok & here
        return ok

    def device(dx, dz):
        return (shot, lax.rem(gx + dx + n_gx, n_gx), lax.rem(sec + dz + n_sec, n_sec), gy)

    side_device = (shot, gx, sec, partner)
    moves = ((1, 0), (-1, 0), (0, 1), (0, -1)) + DIAGONALS

    barrier = pltpu.get_barrier_semaphore()
    count = jnp.int32(1)
    for dx, dz in moves:
        ok = there(dx, dz)
        count += ok.astype(jnp.int32)

        @pl.when(ok)
        def _():
            pl.semaphore_signal(barrier, inc=1, device_id=device(dx, dz), device_id_type=MESH)

    pl.semaphore_signal(barrier, inc=1, device_id=side_device, device_id_type=MESH)

    def load(source, target, i):
        out = []
        for t in range(NT):
            c = pltpu.make_async_copy(
                source.at[:, :, pl.ds(t * LANES, LANES)], target(t), in_sem.at[i * NT + t]
            )
            c.start()
            out.append(c)
        return out

    ins = [
        load(now_h, lambda t: u0.at[t, pl.ds(1, X), rows, :], 0),
        load(tilt_h, lambda t: coef.at[0, t], 1),
        load(aniso_h, lambda t: coef.at[1, t], 2),
        load(courant_h, lambda t: courant.at[t], 3),
        load(before_h, lambda t: before.at[t], 4),
    ]
    refl_in = []
    for t in range(NT):
        c = pltpu.make_async_copy(
            refl_h.at[:, :, :, pl.ds(t * LANES, LANES)], refl.at[t], in_sem.at[5 * NT + t]
        )
        c.start()
        refl_in.append(c)

    def remote(src, dst, e, slot, dev):
        return pltpu.make_async_remote_copy(
            src_ref=src, dst_ref=dst,
            send_sem=send_sem.at[e * SLOTS + slot], recv_sem=recv_sem.at[e * SLOTS + slot],
            device_id=dev, device_id_type=MESH,
        )

    def pad_of(f):
        return (f.shape[1] - X) // 2

    def exchange(f, e, near=True, far=False, skip=0):
        px = pad_of(f)
        every = pl.ds(0, NT)
        xs = pl.ds(px, X)
        out = []
        if near:
            for d, slot in ((1, X_UP), (-1, X_DOWN)):
                src = px + X - 1 if d == 1 else px
                dst = px - 1 if d == 1 else px + X
                out.append((there(d, 0), there(-d, 0), remote(
                    f.at[every, pl.ds(src, 1), rows, :], f.at[every, pl.ds(dst, 1), rows, :],
                    e, slot, device(d, 0))))
            for d, slot in ((1, Z_UP), (-1, Z_DOWN)):
                src = Z0 + Z - 1 if d == 1 else Z0
                dst = Z0 - 1 if d == 1 else Z0 + Z
                out.append((there(0, d), there(0, -d), remote(
                    f.at[every, xs, pl.ds(src, 1), :], f.at[every, xs, pl.ds(dst, 1), :],
                    e, slot, device(0, d))))
            for k, (dx, dz) in enumerate(DIAGONALS):
                sx, tx = (px + X - 1, px - 1) if dx == 1 else (px, px + X)
                sz, tz = (Z0 + Z - 1, Z0 - 1) if dz == 1 else (Z0, Z0 + Z)
                out.append((there(dx, dz), there(-dx, -dz), remote(
                    f.at[every, pl.ds(sx, 1), pl.ds(sz, 1), :],
                    f.at[every, pl.ds(tx, 1), pl.ds(tz, 1), :],
                    e, DIAG + k, device(dx, dz))))
            out.append((None, None, remote(
                f.at[(NT - 1) * (1 - gy), xs, rows, :], f.at[NT, xs, rows, :],
                e, SIDE, side_device)))
        if far:
            size = MARGIN - skip
            for d, slot in ((1, FAR_UP), (-1, FAR_DOWN)):
                src = px + X - MARGIN if d == 1 else px + skip
                dst = px - MARGIN if d == 1 else px + X + skip
                out.append((there(d, 0), there(-d, 0), remote(
                    f.at[every, pl.ds(src, size), rows, :], f.at[every, pl.ds(dst, size), rows, :],
                    e, slot, device(d, 0))))
        return out

    def guarded(ok, act):
        if ok is None:
            act()
        else:
            pl.when(ok)(act)

    sent = []

    def send(copies):
        for ok, _, c in copies:
            guarded(ok, lambda c=c: c.start())
        sent.append(copies)
        return copies

    def receive(copies):
        for _, ok, c in copies:
            guarded(ok, lambda c=c: c.wait_recv())

    def clear(f, near=True):
        px = pad_of(f)
        deep = px
        for d in (1, -1):
            @pl.when(jnp.logical_not(there(d, 0)))
            def _():
                start = px + X if d == 1 else 0

                @pl.loop(0, deep)
                def _(i):
                    for t in range(NT):
                        f[t, start + i] = jnp.zeros(f.shape[2:], f.dtype)

            if near:
                @pl.when(jnp.logical_not(there(0, d)))
                def _():
                    row = Z0 + Z if d == 1 else Z0 - 1

                    @pl.loop(0, X + 2)
                    def _(i):
                        for t in range(NT):
                            f[t, px - 1 + i, pl.ds(row, 1), :] = jnp.zeros((1, LANES), f.dtype)

    lane = lax.broadcasted_iota(jnp.int32, (Z, LANES), 1)
    first, final = lane == 0, lane == LANES - 1
    has_left = jnp.full((Z, LANES), gy, jnp.int32) > 0
    turn = 1 + (LANES - 2) * (1 - gy)

    def step(f, prior, out, forcing=None):
        px = pad_of(f)

        def plane(i):
            c, s, d = [], [], []
            for t in range(NT):
                c.append(f[t, i, rows, :])
                hi = f[t, i, pl.ds(Z0 + 1, Z), :]
                lo = f[t, i, pl.ds(Z0 - 1, Z), :]
                s.append(hi + lo)
                d.append(hi - lo)
            return c, s, d

        def body(x, carry):
            cm, dm, c, s, d = carry
            cp, sp, dp = plane(px + x + 1)
            up = [pltpu.roll(v, 1, 1) for v in c]
            down = [pltpu.roll(v, LANES - 1, 1) for v in c]
            edge = pltpu.roll(f[NT, px + x, rows, :], turn, 1)
            edge_l = jnp.where(has_left, edge, 0.0)
            edge_r = jnp.where(has_left, 0.0, edge)
            for t in range(NT):
                left = jnp.where(first, up[t - 1] if t else edge_l, up[t])
                right = jnp.where(final, down[t + 1] if t < NT - 1 else edge_r, down[t])
                v = coef[0, t, x] * (cp[t] + cm[t])
                v += coef[1, t, x] * s[t]
                v += coef[2, t, x] * (left + right)
                v += coef[3, t, x] * (dp[t] - dm[t])
                v += coef[4, t, x] * c[t]
                if prior is not None:
                    v -= prior(t, x)
                if forcing is not None:
                    v += forcing(t, x)
                out(t, x, v)
            return c, d, cp, sp, dp

        cm, _, dm = plane(px - 1)
        c, s, d = plane(px)
        lax.fori_loop(0, X, body, (cm, dm, c, s, d), unroll=16)

    def reader(f):
        px = pad_of(f)
        return lambda t, x: f[t, px + x, rows, :]

    def writer(f):
        px = pad_of(f)

        def put(t, x, v):
            f[t, px + x, rows, :] = v

        return put

    def source(f, out):
        px = pad_of(f)
        starts = [off_s[h] + px for h in range(noff)]

        def body(x, carry):
            for t in range(NT):
                total = jnp.zeros((Z, LANES), jnp.float32)
                for h in range(noff):
                    total += refl[t, h, x].astype(jnp.float32) * f[t, x + starts[h], rows, :]
                out(t, x, courant[t, x] * total)
            return carry

        lax.fori_loop(0, X, body, 0, unroll=2)

    def plain(f):
        return lambda t, x: f[t, x]

    def put_plain(f):
        def put(t, x, v):
            f[t, x] = v

        return put

    for c in ins[0]:
        c.wait()
    pl.semaphore_wait(barrier, count)
    e0 = send(exchange(u0, 0))
    for k in (1, 2, 3, 4):
        for c in ins[k]:
            c.wait()

    def coefficients(x, carry):
        for t in range(NT):
            ss, cc, sc = trig_products(coef[0, t, x])
            e = coef[1, t, x]
            k = courant[t, x]
            stretch = 1.0 + 2.0 * e
            xx = k * (stretch * cc + ss)
            zz = k * (stretch * ss + cc)
            yy = k * stretch
            coef[0, t, x] = xx
            coef[1, t, x] = zz
            coef[2, t, x] = yy
            coef[3, t, x] = k * e * sc
            coef[4, t, x] = 2.0 - 2.0 * (xx + zz + yy)
        return carry

    lax.fori_loop(0, X, coefficients, 0, unroll=2)
    for f in (u0, u1, u2, u3, u4, u5, w1, w2, w3, w4, w5):
        clear(f)
    clear(u6, near=False)

    receive(e0)
    step(u0, plain(before), writer(u1))
    e1 = send(exchange(u1, 1))
    receive(e1)
    step(u1, reader(u0), writer(u2))
    e2 = send(exchange(u2, 2))
    far2 = send(exchange(u2, 2, near=False, far=True, skip=1))
    receive(e2)
    step(u2, reader(u1), writer(u3))
    e3 = send(exchange(u3, 3))
    for c in refl_in:
        c.wait()
    receive(e3)
    step(u3, reader(u2), writer(u4))
    e4 = send(exchange(u4, 4))
    far4 = send(exchange(u4, 4, near=False, far=True, skip=1))
    receive(far2)
    source(u2, writer(w1))
    g1 = send(exchange(w1, 7))
    receive(e4)
    step(u4, reader(u3), writer(u5))
    e5 = send(exchange(u5, 5))
    receive(g1)
    step(w1, None, writer(w2), reader(w1))
    g2 = send(exchange(w2, 8))
    receive(e5)
    step(u5, reader(u4), writer(u6))
    far6 = send(exchange(u6, 6, near=False, far=True))
    outs = []
    for t in range(NT):
        c = pltpu.make_async_copy(
            u6.at[t, pl.ds(MARGIN, X), rows, :], back_h.at[:, :, pl.ds(t * LANES, LANES)], out_sem.at[t]
        )
        c.start()
        outs.append(c)
    receive(far4)
    source(u4, put_plain(force))
    receive(g2)
    step(w2, reader(w1), writer(w3), plain(force))
    g3 = send(exchange(w3, 9))
    receive(g3)
    step(w3, reader(w2), writer(w4), plain(force))
    g4 = send(exchange(w4, 10))
    receive(far6)
    source(u6, put_plain(force))
    receive(g4)
    step(w4, reader(w3), writer(w5), plain(force))
    g5 = send(exchange(w5, 11))
    receive(g5)
    step(w5, reader(w4), put_plain(last), plain(force))
    for t in range(NT):
        c = pltpu.make_async_copy(
            last.at[t], scat_h.at[:, :, pl.ds(t * LANES, LANES)], out_sem.at[NT + t]
        )
        c.start()
        outs.append(c)
    for copies in sent:
        for ok, _, c in copies:
            guarded(ok, lambda c=c: c.wait_send())
    for c in outs:
        c.wait()


def hand_over(pieces, a, b, a_out, b_out, sem):
    size = a.shape[0] // pieces
    copies = []
    for k, (src, dst) in enumerate(((a, a_out), (b, b_out))):
        for i in range(pieces):
            part = pl.ds(i * size, size)
            copies.append(pltpu.make_async_copy(src.at[part], dst.at[part], sem.at[k * pieces + i]))
    for c in copies:
        c.start()
    for c in copies:
        c.wait()


def shards(sizes, wave_now, wave_before, courant, anisotropy, tilt, reflectivity, offsets):
    X, Z, Y = wave_now.shape
    noff = reflectivity.shape[0]
    NT = Y // LANES
    f32 = jnp.float32
    thin = pltpu.VMEM((NT + 1, X + 2, Z + 2 * Z0, LANES), f32)
    wide = pltpu.VMEM((NT + 1, X + 2 * MARGIN, Z + 2 * Z0, LANES), f32)
    block = pltpu.VMEM((NT, X, Z, LANES), f32)
    exchanges = 12
    any_ = pl.BlockSpec(memory_space=pl.ANY)
    shape = jax.ShapeDtypeStruct(wave_now.shape, f32)
    fields = pl.pallas_call(
        functools.partial(kernel, *sizes, noff),
        out_shape=(shape, shape),
        in_specs=[any_] * 6 + [pl.BlockSpec(memory_space=pltpu.SMEM)],
        out_specs=(any_, any_),
        scratch_shapes=[
            thin, thin, wide, thin, wide, thin, wide,
            thin, thin, thin, thin, thin,
            block,
            pltpu.VMEM((5, NT, X, Z, LANES), f32),
            block,
            pltpu.VMEM((NT, noff, X, Z, LANES), jnp.bfloat16),
            block, block,
            pltpu.SemaphoreType.DMA((6 * NT,)),
            pltpu.SemaphoreType.DMA((2 * NT,)),
            pltpu.SemaphoreType.DMA((exchanges * SLOTS,)),
            pltpu.SemaphoreType.DMA((exchanges * SLOTS,)),
        ],
        compiler_params=pltpu.CompilerParams(
            collective_id=0, has_side_effects=True, vmem_limit_bytes=56 * 1024 * 1024
        ),
    )(wave_now, wave_before, courant, anisotropy, tilt, reflectivity, offsets)
    pieces = 4
    return pl.pallas_call(
        functools.partial(hand_over, pieces),
        out_shape=(shape, shape),
        in_specs=[any_] * 2,
        out_specs=(any_, any_),
        scratch_shapes=[pltpu.SemaphoreType.DMA((2 * pieces,))],
        cost_estimate=pl.CostEstimate(flops=0, bytes_accessed=16 * X * Z * Y, transcendentals=0),
    )(*fields)


def solution(mesh):
    field = P(("shot", "gx"), "section", "gy")
    sizes = tuple(mesh.shape[a] for a in ("gx", "section", "gy"))
    return jax.shard_map(
        functools.partial(shards, sizes),
        mesh=mesh,
        in_specs=(field, field, field, field, field, P(None, ("shot", "gx"), "section", "gy"), P()),
        out_specs=(field, field),
        check_vma=False,
    )
```
